256 devices in a mesh: sens: 32 (over x_lo, z, core), cand: 8 (over x_hi, y).
Axes of the slice: x: 4 (x_hi: 2, x_lo: 2; x = x_hi * 2 + x_lo), y: 4, z: 8, core: 2. Of those that a mesh axis runs over, the one named last changes fastest.
Arguments:
- jacobian: bfloat16 [8192, 131072], P('sens', 'cand'), may hold values from -0.015625 to 0.015625
- weights: float32 [2, 8192], P(None, 'sens'), may hold values from 1 to 10
- blocks: float32 [2, 16, 131072], P(None, None, 'cand'), may hold values from -6 to 6
Outputs:
- curvature: float32 [2, 16, 131072], P(None, None, 'cand')
The draws below stay inside these ranges and needn't reach their ends.
All inputs are finite; a program needn't handle non-finite values.
Results may differ from the reference program's by a relative error of at most 0.004.
Values sent between devices are 32-bit elements; how exact they have to be, the bound alone decides.
No kernel may reach another device: no remote copies, remote signals or barrier semaphores. Data moves between devices by JAX's collectives and lax.ppermute only.
A program may use at most 64 MiB of HBM per device.

```python
import math
import jax
import jax.numpy as jnp
from jax import lax

NCAND = 131072
K = 16
ROWS_DEV = 256
NROWS = 8192
N_SENS = 32


def level_of(stream_key, extent, split, least, top_value):
    def one(position, shards_of):
        draws = jax.random.uniform(jax.random.fold_in(jax.random.fold_in(stream_key, 6), position), (shards_of,), jnp.float32, least / len(split), top_value / len(split))
        return jnp.repeat(jnp.exp(draws), extent[position] // shards_of).reshape((-1,) + (1,) * (len(extent) - position - 1))

    level = one(*split[0])
    for cut in split[1:]:
        level = level * one(*cut)
    return level


def bell_draw(rng, extent, spread, limit, pieces=(), dtype=jnp.bfloat16):
    gain = level_of(rng, extent, pieces, -0.22, 0.18) if pieces else 1.0
    entries = jax.random.normal(rng, extent, jnp.float32) * spread * gain
    return jnp.minimum(jnp.maximum(entries, -limit), limit).astype(dtype)


def setup_inputs(seed: int = 0) -> dict:
    arg_keys = jax.random.split(jax.random.key(seed), 4)
    jacobian = bell_draw(arg_keys[0], (NROWS, NCAND), NCAND ** -0.5, 0.015625, ((0, 32), (1, 8)))
    weights = jnp.clip(jnp.exp(math.log(10.0) - 2.3025851 * jax.random.uniform(arg_keys[1], (2, NROWS), jnp.float32) ** level_of(arg_keys[1], (2, NROWS), ((1, 32),), -0.2, 0.2)), 1.0, 10.0)
    blocks = bell_draw(arg_keys[2], (2, K, NCAND), 1.0, 6.0, ((2, 8),), jnp.float32)
    return dict(jacobian=jacobian, weights=weights, blocks=blocks)


def reference(jacobian, weights, blocks):
    directions = blocks.astype(jnp.bfloat16).astype(jnp.float32)
    stacked = directions.reshape(2 * K, NCAND)
    row_blocks = jacobian.reshape(N_SENS, ROWS_DEV, NCAND)
    weight_blocks = jnp.transpose(weights.reshape(2, N_SENS, ROWS_DEV), (1, 0, 2))

    def step(total, inputs):
        rows, row_weights = inputs
        rows32 = rows.astype(jnp.float32)
        predicted = jnp.dot(stacked, rows32.T, preferred_element_type=jnp.float32, precision=lax.Precision.HIGHEST)
        predicted = predicted.reshape(2, K, ROWS_DEV)
        weighted = (row_weights[:, None, :] * predicted).astype(jnp.bfloat16).astype(jnp.float32)
        term = jnp.dot(weighted.reshape(2 * K, ROWS_DEV), rows32, preferred_element_type=jnp.float32, precision=lax.Precision.HIGHEST)
        return total + term, None

    total, unused = lax.scan(step, jnp.zeros((2 * K, NCAND), jnp.float32), (row_blocks, weight_blocks))
    return total.reshape(2, K, NCAND)
```

```python
import functools

import jax
import jax.numpy as jnp
from jax import lax
from jax.experimental import pallas as pl
from jax.experimental.pallas import tpu as pltpu
from jax.sharding import PartitionSpec as P

N_XL, N_Z, N_CORE = 2, 8, 2
N_SENS = N_XL * N_Z * N_CORE
N_XH, N_Y = 2, 4
N_CAND = N_XH * N_Y
PIECES = 2
MIB = 1 << 20


def sens_id(xl, z, core):
    return (xl * N_Z + z) * N_CORE + core


def sens_perm(move):
    pairs = []
    for xl in range(N_XL):
        for z in range(N_Z):
            for core in range(N_CORE):
                pairs.append((sens_id(xl, z, core), sens_id(*move(xl, z, core))))
    return pairs


CORE_SWAP = sens_perm(lambda xl, z, core: (xl, z, 1 - core))
X_SWAP = sens_perm(lambda xl, z, core: (1 - xl, z, core))
Z_SHIFT = [sens_perm(lambda xl, z, core, k=k: (xl, (z + k) % N_Z, core)) for k in range(N_Z)]
CAND_SHIFT = [
    [
        (xh * N_Y + y, ((xh + a) % N_XH) * N_Y + (y + b) % N_Y)
        for xh in range(N_XH)
        for y in range(N_Y)
    ]
    for a in range(N_XH)
    for b in range(N_Y)
]


def predict_kernel(blocks_ref, jac_ref, out_ref):
    @pl.when(pl.program_id(0) == 0)
    def _():
        out_ref[...] = jnp.zeros_like(out_ref)

    directions = blocks_ref[...].astype(jnp.bfloat16)
    out_ref[...] += lax.dot_general(
        directions, jac_ref[...], (((1,), (1,)), ((), ())), preferred_element_type=jnp.float32
    )


def predict(blocks, jacobian):
    k, ncols = blocks.shape
    rows = jacobian.shape[0]
    width = 2048
    return pl.pallas_call(
        predict_kernel,
        grid=(ncols // width,),
        in_specs=[
            pl.BlockSpec((k, width), lambda i: (0, i)),
            pl.BlockSpec((rows, width), lambda i: (0, i)),
        ],
        out_specs=pl.BlockSpec((k, rows), lambda i: (0, 0)),
        out_shape=jax.ShapeDtypeStruct((k, rows), jnp.float32),
        compiler_params=pltpu.CompilerParams(vmem_limit_bytes=16 * MIB),
        cost_estimate=pl.CostEstimate(
            flops=2 * k * ncols * rows, bytes_accessed=2 * rows * ncols, transcendentals=0
        ),
    )(blocks, jacobian)


def weigh_kernel(weights_ref, *refs):
    parts, out_ref = refs[:-1], refs[-1]
    total = parts[0][...]
    for part in parts[1:]:
        total = total + part[...]
    half = total.shape[0] // 2
    for p in range(2):
        rows = pl.ds(p * half, half)
        out_ref[rows, :] = (
            weights_ref[p : p + 1, :] * total[p * half : (p + 1) * half]
        ).astype(jnp.bfloat16)


def weigh(weights, parts):
    return pl.pallas_call(
        weigh_kernel,
        out_shape=jax.ShapeDtypeStruct(parts[0].shape, jnp.bfloat16),
        compiler_params=pltpu.CompilerParams(vmem_limit_bytes=4 * MIB),
    )(weights, *parts)


def product_kernel(where_ref, weighted_ref, jac_ref, sibling_ref, across_ref, mine_ref):
    step = pl.program_id(0)
    z = where_ref[2]
    chunk = mine_ref.shape[-1]

    def fill(dst):
        for zz in range(N_Z):
            dst[lax.rem(zz + N_Z - z, N_Z)] = jnp.dot(
                weighted_ref[...],
                jac_ref[:, zz * chunk : (zz + 1) * chunk],
                preferred_element_type=jnp.float32,
            )

    @pl.when(step < 2)
    def _():
        fill(sibling_ref.at[step])

    @pl.when(step == 2)
    def _():
        fill(across_ref)

    @pl.when(step == 3)
    def _():
        fill(mine_ref)


def product(where, weighted, jacobian, piece):
    k, rows = weighted.shape
    ncols = jacobian.shape[1]
    chunk = ncols // (PIECES * N_SENS)

    def jac_map(i, where_ref):
        core, xl = where_ref[0], where_ref[1]
        core = jnp.where(i < 2, 1 - core, core)
        xl = jnp.where((i == 0) | (i == 3), xl, 1 - xl)
        return 0, piece * 4 + core * 2 + xl

    vmem = pl.BlockSpec(memory_space=pltpu.VMEM)
    f32 = jnp.float32
    return pl.pallas_call(
        product_kernel,
        grid_spec=pltpu.PrefetchScalarGridSpec(
            num_scalar_prefetch=1,
            grid=(4,),
            in_specs=[vmem, pl.BlockSpec((rows, N_Z * chunk), jac_map)],
            out_specs=[vmem, vmem, vmem],
        ),
        out_shape=[
            jax.ShapeDtypeStruct((2, N_Z, k, chunk), f32),
            jax.ShapeDtypeStruct((N_Z, k, chunk), f32),
            jax.ShapeDtypeStruct((N_Z, k, chunk), f32),
        ],
        compiler_params=pltpu.CompilerParams(vmem_limit_bytes=16 * MIB),
        cost_estimate=pl.CostEstimate(
            flops=2 * k * ncols * rows // PIECES,
            bytes_accessed=2 * rows * ncols // PIECES,
            transcendentals=0,
        ),
    )(where, weighted, jacobian)


def assemble_kernel(where_ref, *refs):
    out_ref = refs[-1]
    core, xl, z = where_ref[0], where_ref[1], where_ref[2]
    chunk = refs[0].shape[-1]
    for piece in range(PIECES):
        own_mine, own_across, sib = refs[3 * piece : 3 * piece + 3]
        for j in range(N_Z):
            zz = lax.rem(z + N_Z - j, N_Z)
            for c, x, value in (
                (core, xl, own_mine[j]),
                (core, 1 - xl, own_across[j]),
                (1 - core, xl, sib[0, j]),
                (1 - core, 1 - xl, sib[1, j]),
            ):
                at = ((piece * 4 + c * 2 + x) * N_Z + zz) * chunk
                out_ref[:, pl.ds(pl.multiple_of(at, chunk), chunk)] = value


def assemble(where, parts, ncols):
    k = parts[0].shape[1]
    vmem = pl.BlockSpec(memory_space=pltpu.VMEM)
    return pl.pallas_call(
        assemble_kernel,
        in_specs=[pl.BlockSpec(memory_space=pltpu.SMEM)] + [vmem] * len(parts),
        out_specs=vmem,
        out_shape=jax.ShapeDtypeStruct((k, ncols), jnp.float32),
        compiler_params=pltpu.CompilerParams(vmem_limit_bytes=16 * MIB),
    )(where, *parts)


def local(jacobian, weights, blocks):
    p, k, ncols = blocks.shape
    me = lax.axis_index("sens")
    where = jnp.stack([me % N_CORE, me // (N_CORE * N_Z), (me // N_CORE) % N_Z]).astype(jnp.int32)

    predicted = predict(blocks.reshape(p * k, ncols), jacobian)
    parts = [predicted] + [lax.ppermute(predicted, "cand", perm) for perm in CAND_SHIFT[1:]]
    weighted = weigh(weights, parts)

    gathered = []
    for piece in range(PIECES):
        to_sibling, to_across, mine = product(where, weighted, jacobian, piece)
        from_sibling = lax.ppermute(to_sibling, "sens", CORE_SWAP)
        from_across = lax.ppermute(to_across + from_sibling[1], "sens", X_SWAP)
        own = mine + from_sibling[0] + from_across
        total = own[0]
        for shift in range(1, N_Z):
            total = total + lax.ppermute(own[shift], "sens", Z_SHIFT[shift])
        column = jnp.stack(
            [total] + [lax.ppermute(total, "sens", Z_SHIFT[shift]) for shift in range(1, N_Z)]
        )
        across = lax.ppermute(column, "sens", X_SWAP)
        sibling = lax.ppermute(jnp.stack([column, across]), "sens", CORE_SWAP)
        gathered += [column, across, sibling]
    return assemble(where, gathered, ncols).reshape(p, k, ncols)


def solution(mesh):
    return jax.shard_map(
        local,
        mesh=mesh,
        in_specs=(P("sens", "cand"), P(None, "sens"), P(None, None, "cand")),
        out_specs=P(None, None, "cand"),
        check_vma=False,
    )
```

```python
import jax
import jax.numpy as jnp
from jax import lax
from jax.experimental import pallas as pl
from jax.experimental.pallas import tpu as pltpu
from jax.sharding import PartitionSpec as P

N_CORE = 2
N_Z = 8
N_SENS = 32
N_CAND = 8
SLOTS = 4
STREAMS = 1
STEPS = 8
MIB = 1 << 20

STEP_OF_EVEN = (1, -1, 3)


def z_pairs(stage):
    pairs = []
    for s in range(N_SENS):
        core, z, xl = s % N_CORE, (s // N_CORE) % N_Z, s // (N_CORE * N_Z)
        sign = 1 if (z - core) % 2 == 0 else -1
        to = (z + sign * STEP_OF_EVEN[stage]) % N_Z
        pairs.append((s, (xl * N_Z + to) * N_CORE + core))
    return pairs


NEAR, NEXT, FAR = z_pairs(0), z_pairs(1), z_pairs(2)
CORE_SWAP = [(s, s ^ 1) for s in range(N_SENS)]
X_SWAP = [(s, s ^ 16) for s in range(N_SENS)]
CAND_STAGES = [[(c, c ^ flip) for c in range(N_CAND)] for flip in (1, 3, 4)]
PAIR_OF_SLOT = (0, 2, -1, 1)

VMEM = pl.BlockSpec(memory_space=pltpu.VMEM)
SMEM = pl.BlockSpec(memory_space=pltpu.SMEM)
HBM = pl.BlockSpec(memory_space=pltpu.HBM)


def slot_columns(me, core, slot, stream, width):
    place = lax.rem(lax.div(me, N_CORE) + N_Z - core, N_Z)
    odd = lax.rem(place, 2)
    pair = lax.div(place + odd * (2 * N_Z - 3), 2)
    pair = lax.rem(pair + 2 * N_Z + (1 - 2 * odd) * PAIR_OF_SLOT[slot], SLOTS)
    block = (core * STREAMS + stream) * SLOTS + pair
    return pl.ds(pl.multiple_of(block * width, width), width)


def predict_kernel(me_ref, blocks_ref, jac_ref, out_ref):
    width = jac_ref.shape[1] // STEPS
    total = jnp.zeros(out_ref.shape, jnp.float32)
    for step in range(STEPS):
        cols = slice(step * width, (step + 1) * width)
        total += lax.dot_general(
            blocks_ref[:, cols].astype(jnp.bfloat16),
            jac_ref[:, cols],
            (((1,), (1,)), ((), ())),
            preferred_element_type=jnp.float32,
        )
    out_ref[...] = total


def predict(me, blocks, jacobian):
    k, ncols = blocks.shape
    rows = jacobian.shape[0]
    return pl.pallas_call(
        predict_kernel,
        in_specs=[SMEM, VMEM, VMEM],
        out_specs=VMEM,
        out_shape=jax.ShapeDtypeStruct((k, rows), jnp.float32),
        compiler_params=pltpu.CompilerParams(vmem_limit_bytes=24 * MIB),
        cost_estimate=pl.CostEstimate(
            flops=2 * k * ncols * rows, bytes_accessed=2 * rows * ncols, transcendentals=0
        ),
    )(me, blocks, jacobian)


def product(me, weighted, held, other_core, slots, stream):
    k, rows = weighted.shape
    width = held.shape[1] // (N_CORE * SLOTS * STREAMS)

    def kernel(me_ref, weighted_ref, held_ref, out_ref):
        core = lax.rem(me_ref[0], N_CORE)
        core = 1 - core if other_core else core
        for i, slot in enumerate(slots):
            out_ref[i] = jnp.dot(
                weighted_ref[...],
                held_ref[:, slot_columns(me_ref[0], core, slot, stream, width)],
                preferred_element_type=jnp.float32,
            )

    return pl.pallas_call(
        kernel,
        in_specs=[SMEM, VMEM, VMEM],
        out_specs=VMEM,
        out_shape=jax.ShapeDtypeStruct((len(slots), k, width), jnp.float32),
        compiler_params=pltpu.CompilerParams(vmem_limit_bytes=24 * MIB),
        cost_estimate=pl.CostEstimate(
            flops=2 * k * len(slots) * width * rows,
            bytes_accessed=2 * rows * len(slots) * width,
            transcendentals=0,
        ),
    )(me, weighted, held)


def assemble(me, streams, ncols):
    k, width = streams[0][0].shape[-2:]
    per_stream = len(streams[0])

    def kernel(me_ref, *refs):
        out_ref = refs[-1]
        core = lax.rem(me_ref[0], N_CORE)
        for stream in range(STREAMS):
            parts = refs[stream * per_stream : (stream + 1) * per_stream]
            for owner, (low, high) in ((core, parts[:2]), (1 - core, parts[2:])):
                for slot in range(SLOTS):
                    ref = low if slot < 2 else high
                    cols = slot_columns(me_ref[0], owner, slot, stream, width)
                    out_ref[:, cols] = ref[slot % 2]

    operands = [part for parts in streams for part in parts]
    return pl.pallas_call(
        kernel,
        in_specs=[SMEM] + [VMEM] * len(operands),
        out_specs=VMEM,
        out_shape=jax.ShapeDtypeStruct((k, ncols), jnp.float32),
        compiler_params=pltpu.CompilerParams(vmem_limit_bytes=16 * MIB),
    )(me, *operands)


def local(jacobian, weights, blocks):
    p, k, ncols = blocks.shape
    me = lax.axis_index("sens").astype(jnp.int32).reshape(1)

    def swap(value, pairs):
        return lax.ppermute(value, "sens", pairs)

    predicted = predict(me, blocks.reshape(p * k, ncols), jacobian)
    held = jacobian
    for pairs in CAND_STAGES:
        predicted = predicted + lax.ppermute(predicted, "cand", pairs)
    weighted = weights[:, None, :] * predicted.reshape(p, k, -1)
    weighted = weighted.reshape(p * k, -1).astype(jnp.bfloat16)

    streams = []
    for stream in range(STREAMS):
        high = swap(product(me, weighted, held, True, (2, 3), stream), CORE_SWAP)
        high = high + product(me, weighted, held, False, (2, 3), stream)
        near = swap(high, NEAR)
        low = swap(product(me, weighted, held, True, (0, 1), stream), CORE_SWAP)
        low = low + product(me, weighted, held, False, (0, 1), stream)
        total = low[0] + near[0] + swap(low[1] + near[1], NEXT)
        total = total + swap(total, FAR)
        total = total + swap(total, X_SWAP)
        low = jnp.stack([total, swap(total, NEXT)])
        high = swap(low, NEAR)
        streams.append((low, high, swap(low, CORE_SWAP), swap(high, CORE_SWAP)))
    return assemble(me, streams, ncols).reshape(p, k, ncols)


def solution(mesh):
    return jax.shard_map(
        local,
        mesh=mesh,
        in_specs=(P("sens", "cand"), P(None, "sens"), P(None, None, "cand")),
        out_specs=P(None, None, "cand"),
        check_vma=False,
    )
```

```python
import jax
import jax.numpy as jnp
from jax import lax
from jax.experimental import pallas as pl
from jax.experimental.pallas import tpu as pltpu
from jax.sharding import PartitionSpec as P

N_CORE = 2
N_Z = 8
N_SENS = 32
N_CAND = 8
SLOTS = 4
STREAMS = 2
STEPS = 8
MIB = 1 << 20

STEP_OF_EVEN = (1, -1, 3)


def z_pairs(stage):
    pairs = []
    for s in range(N_SENS):
        core, z, xl = s % N_CORE, (s // N_CORE) % N_Z, s // (N_CORE * N_Z)
        sign = 1 if (z - core) % 2 == 0 else -1
        to = (z + sign * STEP_OF_EVEN[stage]) % N_Z
        pairs.append((s, (xl * N_Z + to) * N_CORE + core))
    return pairs


NEAR, NEXT, FAR = z_pairs(0), z_pairs(1), z_pairs(2)
CORE_SWAP = [(s, s ^ 1) for s in range(N_SENS)]
X_SWAP = [(s, s ^ 16) for s in range(N_SENS)]
CAND_STAGES = [[(c, c ^ flip) for c in range(N_CAND)] for flip in (1, 3, 4)]
X_FIRST = (False, False)
SUMS = ((FAR, NEXT), (NEXT, FAR))

VMEM = pl.BlockSpec(memory_space=pltpu.VMEM)
SMEM = pl.BlockSpec(memory_space=pltpu.SMEM)
HBM = pl.BlockSpec(memory_space=pltpu.HBM)


def slot_columns(me, core, slot, stream, width):
    place = lax.rem(lax.div(me, N_CORE) + N_Z - core, N_Z)
    half = lax.rem(lax.div(place + 1, 2), 2)
    xl = lax.div(me, N_CORE * N_Z)
    first, second = slot // 2, slot % 2
    if X_FIRST[stream]:
        first, second = second, first
    half = 1 - half if first else half
    xl = 1 - xl if second else xl
    block = (core * STREAMS + stream) * SLOTS + 2 * half + xl
    return pl.ds(pl.multiple_of(block * width, width), width)


def predict_kernel(me_ref, blocks_ref, jac_ref, out_ref):
    width = jac_ref.shape[1] // STEPS
    total = jnp.zeros(out_ref.shape, jnp.float32)
    for step in range(STEPS):
        cols = slice(step * width, (step + 1) * width)
        total += lax.dot_general(
            blocks_ref[:, cols].astype(jnp.bfloat16),
            jac_ref[:, cols],
            (((1,), (1,)), ((), ())),
            preferred_element_type=jnp.float32,
        )
    out_ref[...] = total


def predict(me, blocks, jacobian):
    k, ncols = blocks.shape
    rows = jacobian.shape[0]
    return pl.pallas_call(
        predict_kernel,
        in_specs=[SMEM, VMEM, VMEM],
        out_specs=VMEM,
        out_shape=jax.ShapeDtypeStruct((k, rows), jnp.float32),
        compiler_params=pltpu.CompilerParams(vmem_limit_bytes=24 * MIB),
        cost_estimate=pl.CostEstimate(
            flops=2 * k * ncols * rows, bytes_accessed=2 * rows * ncols, transcendentals=0
        ),
    )(me, blocks, jacobian)


def product(me, weighted, held, other_core, slots, stream):
    k, rows = weighted.shape
    width = held.shape[1] // (N_CORE * SLOTS * STREAMS)

    def kernel(me_ref, weighted_ref, held_ref, out_ref):
        core = lax.rem(me_ref[0], N_CORE)
        core = 1 - core if other_core else core
        for i, slot in enumerate(slots):
            out_ref[i] = jnp.dot(
                weighted_ref[...],
                held_ref[:, slot_columns(me_ref[0], core, slot, stream, width)],
                preferred_element_type=jnp.float32,
            )

    return pl.pallas_call(
        kernel,
        in_specs=[SMEM, VMEM, VMEM],
        out_specs=VMEM,
        out_shape=jax.ShapeDtypeStruct((len(slots), k, width), jnp.float32),
        compiler_params=pltpu.CompilerParams(vmem_limit_bytes=24 * MIB),
        cost_estimate=pl.CostEstimate(
            flops=2 * k * len(slots) * width * rows,
            bytes_accessed=2 * rows * len(slots) * width,
            transcendentals=0,
        ),
    )(me, weighted, held)


def assemble(me, streams, ncols):
    k, width = streams[0][0].shape[-2:]
    per_stream = len(streams[0])

    def kernel(me_ref, *refs):
        out_ref = refs[-1]
        core = lax.rem(me_ref[0], N_CORE)
        for stream in range(STREAMS):
            parts = refs[stream * per_stream : (stream + 1) * per_stream]
            for owner, (low, high) in ((core, parts[:2]), (1 - core, parts[2:])):
                for slot in range(SLOTS):
                    ref = low if slot < 2 else high
                    cols = slot_columns(me_ref[0], owner, slot, stream, width)
                    out_ref[:, cols] = ref[slot % 2]

    operands = [part for parts in streams for part in parts]
    return pl.pallas_call(
        kernel,
        in_specs=[SMEM] + [VMEM] * len(operands),
        out_specs=VMEM,
        out_shape=jax.ShapeDtypeStruct((k, ncols), jnp.float32),
        compiler_params=pltpu.CompilerParams(vmem_limit_bytes=16 * MIB),
    )(me, *operands)


def local(jacobian, weights, blocks):
    p, k, ncols = blocks.shape
    me = lax.axis_index("sens").astype(jnp.int32).reshape(1)

    def swap(value, pairs):
        return lax.ppermute(value, "sens", pairs)

    predicted = predict(me, blocks.reshape(p * k, ncols), jacobian)
    held = jacobian
    def flip(value, bits):
        return lax.ppermute(value, "cand", [(c, c ^ bits) for c in range(N_CAND)])

    predicted = predicted + flip(predicted, 1) + (flip(predicted, 3) + flip(predicted, 2))
    predicted = predicted + flip(predicted, 4)
    weighted = weights[:, None, :] * predicted.reshape(p, k, -1)
    weighted = weighted.reshape(p * k, -1).astype(jnp.bfloat16)

    streams = []
    for stream in range(STREAMS):
        first, second = (X_SWAP, NEAR) if X_FIRST[stream] else (NEAR, X_SWAP)
        high = swap(product(me, weighted, held, True, (2, 3), stream), CORE_SWAP)
        high = high + product(me, weighted, held, False, (2, 3), stream)
        high = swap(high, first)
        low = swap(product(me, weighted, held, True, (0, 1), stream), CORE_SWAP)
        low = low + product(me, weighted, held, False, (0, 1), stream)
        total = low[0] + high[0] + swap(low[1] + high[1], second)
        for pairs in SUMS[stream]:
            total = total + swap(total, pairs)
        low = jnp.stack([total, swap(total, second)])
        high = swap(low, first)
        streams.append((low, high, swap(low, CORE_SWAP), swap(high, CORE_SWAP)))
    return assemble(me, streams, ncols).reshape(p, k, ncols)


def solution(mesh):
    return jax.shard_map(
        local,
        mesh=mesh,
        in_specs=(P("sens", "cand"), P(None, "sens"), P(None, None, "cand")),
        out_specs=P(None, None, "cand"),
        check_vma=False,
    )
```

```python
import jax
import jax.numpy as jnp
from jax import lax
from jax.experimental import pallas as pl
from jax.experimental.pallas import tpu as pltpu
from jax.sharding import PartitionSpec as P

N_CORE = 2
N_Z = 8
N_SENS = 32
N_CAND = 8
SLOTS = 4
STREAMS = 2
STEPS = 8
MIB = 1 << 20

STEP_OF_EVEN = (1, -1, 3)


def z_pairs(stage):
    pairs = []
    for s in range(N_SENS):
        core, z, xl = s % N_CORE, (s // N_CORE) % N_Z, s // (N_CORE * N_Z)
        sign = 1 if (z - core) % 2 == 0 else -1
        to = (z + sign * STEP_OF_EVEN[stage]) % N_Z
        pairs.append((s, (xl * N_Z + to) * N_CORE + core))
    return pairs


NEAR, NEXT, FAR = z_pairs(0), z_pairs(1), z_pairs(2)
CORE_SWAP = [(s, s ^ 1) for s in range(N_SENS)]
X_SWAP = [(s, s ^ 16) for s in range(N_SENS)]
CAND_STAGES = [[(c, c ^ flip) for c in range(N_CAND)] for flip in (1, 3, 4)]
X_FIRST = (False, False)
SUMS = ((FAR, NEXT), (NEXT, FAR))

VMEM = pl.BlockSpec(memory_space=pltpu.VMEM)
SMEM = pl.BlockSpec(memory_space=pltpu.SMEM)
HBM = pl.BlockSpec(memory_space=pltpu.HBM)


def slot_columns(me, core, slot, stream, width):
    place = lax.rem(lax.div(me, N_CORE) + N_Z - core, N_Z)
    half = lax.rem(lax.div(place + 1, 2), 2)
    xl = lax.div(me, N_CORE * N_Z)
    first, second = slot // 2, slot % 2
    if X_FIRST[stream]:
        first, second = second, first
    half = 1 - half if first else half
    xl = 1 - xl if second else xl
    block = (core * STREAMS + stream) * SLOTS + 2 * half + xl
    return pl.ds(pl.multiple_of(block * width, width), width)


def predict_kernel(
    me_ref, blocks_ref, jac_ref, out_ref, held_ref, blocks_buf, blocks_sem, jac_sem
):
    width = jac_ref.shape[1] // STEPS

    def columns(step):
        return pl.ds(pl.multiple_of(step * width, width), width)

    def copies(step):
        cols = columns(step)
        return (
            pltpu.make_async_copy(
                blocks_ref.at[:, cols], blocks_buf.at[:, cols], blocks_sem.at[step]
            ),
            pltpu.make_async_copy(jac_ref.at[:, cols], held_ref.at[:, cols], jac_sem.at[step]),
        )

    for step in range(STEPS):
        for copy in copies(step):
            copy.start()

    def add(step, total):
        for copy in copies(step):
            copy.wait()
        cols = columns(step)
        return total + lax.dot_general(
            blocks_buf[:, cols].astype(jnp.bfloat16),
            held_ref[:, cols],
            (((1,), (1,)), ((), ())),
            preferred_element_type=jnp.float32,
        )

    out_ref[...] = lax.fori_loop(0, STEPS, add, jnp.zeros(out_ref.shape, jnp.float32))


def predict(me, blocks, jacobian):
    k, ncols = blocks.shape
    rows = jacobian.shape[0]
    return pl.pallas_call(
        predict_kernel,
        in_specs=[SMEM, HBM, HBM],
        out_specs=[VMEM, VMEM],
        out_shape=[
            pltpu.VMEM((k, rows), jnp.float32),
            pltpu.VMEM(jacobian.shape, jacobian.dtype),
        ],
        scratch_shapes=[
            pltpu.VMEM((k, ncols), jnp.float32),
            pltpu.SemaphoreType.DMA((STEPS,)),
            pltpu.SemaphoreType.DMA((STEPS,)),
        ],
        compiler_params=pltpu.CompilerParams(vmem_limit_bytes=48 * MIB),
        cost_estimate=pl.CostEstimate(
            flops=2 * k * ncols * rows, bytes_accessed=2 * rows * ncols, transcendentals=0
        ),
    )(me, blocks, jacobian)


def product(me, weighted, held, other_core, slots, stream):
    k, rows = weighted.shape
    width = held.shape[1] // (N_CORE * SLOTS * STREAMS)

    def kernel(me_ref, weighted_ref, held_ref, out_ref):
        core = lax.rem(me_ref[0], N_CORE)
        core = 1 - core if other_core else core
        for i, slot in enumerate(slots):
            out_ref[i] = jnp.dot(
                weighted_ref[...],
                held_ref[:, slot_columns(me_ref[0], core, slot, stream, width)],
                preferred_element_type=jnp.float32,
            )

    return pl.pallas_call(
        kernel,
        in_specs=[SMEM, VMEM, VMEM],
        out_specs=VMEM,
        out_shape=jax.ShapeDtypeStruct((len(slots), k, width), jnp.float32),
        compiler_params=pltpu.CompilerParams(vmem_limit_bytes=24 * MIB),
        cost_estimate=pl.CostEstimate(
            flops=2 * k * len(slots) * width * rows,
            bytes_accessed=2 * rows * len(slots) * width,
            transcendentals=0,
        ),
    )(me, weighted, held)


def assemble(me, streams, ncols):
    k, width = streams[0][0].shape[-2:]
    per_stream = len(streams[0])

    def kernel(me_ref, *refs):
        out_ref = refs[-1]
        core = lax.rem(me_ref[0], N_CORE)
        for stream in range(STREAMS):
            parts = refs[stream * per_stream : (stream + 1) * per_stream]
            for owner, (low, high) in ((core, parts[:2]), (1 - core, parts[2:])):
                for slot in range(SLOTS):
                    ref = low if slot < 2 else high
                    cols = slot_columns(me_ref[0], owner, slot, stream, width)
                    out_ref[:, cols] = ref[slot % 2]

    operands = [part for parts in streams for part in parts]
    return pl.pallas_call(
        kernel,
        in_specs=[SMEM] + [VMEM] * len(operands),
        out_specs=VMEM,
        out_shape=jax.ShapeDtypeStruct((k, ncols), jnp.float32),
        compiler_params=pltpu.CompilerParams(vmem_limit_bytes=16 * MIB),
    )(me, *operands)


def local(jacobian, weights, blocks):
    p, k, ncols = blocks.shape
    me = lax.axis_index("sens").astype(jnp.int32).reshape(1)

    def swap(value, pairs):
        return lax.ppermute(value, "sens", pairs)

    predicted, held = predict(me, blocks.reshape(p * k, ncols), jacobian)
    def flip(value, bits):
        return lax.ppermute(value, "cand", [(c, c ^ bits) for c in range(N_CAND)])

    predicted = predicted + flip(predicted, 1) + (flip(predicted, 3) + flip(predicted, 2))
    predicted = predicted + flip(predicted, 4)
    weighted = weights[:, None, :] * predicted.reshape(p, k, -1)
    weighted = weighted.reshape(p * k, -1).astype(jnp.bfloat16)

    streams = []
    for stream in range(STREAMS):
        first, second = (X_SWAP, NEAR) if X_FIRST[stream] else (NEAR, X_SWAP)
        high = swap(product(me, weighted, held, True, (2, 3), stream), CORE_SWAP)
        high = high + product(me, weighted, held, False, (2, 3), stream)
        high = swap(high, first)
        low = swap(product(me, weighted, held, True, (0, 1), stream), CORE_SWAP)
        low = low + product(me, weighted, held, False, (0, 1), stream)
        total = low[0] + high[0] + swap(low[1] + high[1], second)
        for pairs in SUMS[stream]:
            total = total + swap(total, pairs)
        own = swap(total, first)
        other = swap(total, second)
        low = jnp.stack([total, other])
        high = jnp.stack([own, swap(other, first)])
        streams.append((low, high, swap(low, CORE_SWAP), swap(high, CORE_SWAP)))
    return assemble(me, streams, ncols).reshape(p, k, ncols)


def solution(mesh):
    return jax.shard_map(
        local,
        mesh=mesh,
        in_specs=(P("sens", "cand"), P(None, "sens"), P(None, None, "cand")),
        out_specs=P(None, None, "cand"),
        check_vma=False,
    )
```

```python
import jax
import jax.numpy as jnp
from jax import lax
from jax.experimental import pallas as pl
from jax.experimental.pallas import tpu as pltpu
from jax.sharding import PartitionSpec as P

N_CORE = 2
N_Z = 8
N_SENS = 32
N_CAND = 8
SLOTS = 4
STREAMS = 2
STEPS = 8
MIB = 1 << 20

STEP_OF_EVEN = (1, -1, 3)


def z_pairs(stage):
    pairs = []
    for s in range(N_SENS):
        core, z, xl = s % N_CORE, (s // N_CORE) % N_Z, s // (N_CORE * N_Z)
        sign = 1 if (z - core) % 2 == 0 else -1
        to = (z + sign * STEP_OF_EVEN[stage]) % N_Z
        pairs.append((s, (xl * N_Z + to) * N_CORE + core))
    return pairs


NEAR, NEXT, FAR = z_pairs(0), z_pairs(1), z_pairs(2)
CORE_SWAP = [(s, s ^ 1) for s in range(N_SENS)]
X_SWAP = [(s, s ^ 16) for s in range(N_SENS)]
CAND_STAGES = [[(c, c ^ flip) for c in range(N_CAND)] for flip in (1, 3, 4)]
X_FIRST = (False, False)
SUMS = ((FAR, NEXT), (NEXT, FAR))

VMEM = pl.BlockSpec(memory_space=pltpu.VMEM)
SMEM = pl.BlockSpec(memory_space=pltpu.SMEM)
HBM = pl.BlockSpec(memory_space=pltpu.HBM)
ANY = pl.BlockSpec(memory_space=pl.ANY)


def slot_columns(me, core, slot, stream, width):
    place = lax.rem(lax.div(me, N_CORE) + N_Z - core, N_Z)
    half = lax.rem(lax.div(place + 1, 2), 2)
    xl = lax.div(me, N_CORE * N_Z)
    first, second = slot // 2, slot % 2
    if X_FIRST[stream]:
        first, second = second, first
    half = 1 - half if first else half
    xl = 1 - xl if second else xl
    block = (core * STREAMS + stream) * SLOTS + 2 * half + xl
    return pl.ds(pl.multiple_of(block * width, width), width)


def predict_kernel(
    me_ref, blocks_ref, jac_ref, out_ref, held_ref, blocks_buf, blocks_sem, jac_sem
):
    width = jac_ref.shape[1] // STEPS

    def columns(step):
        return pl.ds(pl.multiple_of(step * width, width), width)

    def copies(step):
        cols = columns(step)
        return (
            pltpu.make_async_copy(
                blocks_ref.at[:, cols], blocks_buf.at[:, cols], blocks_sem.at[step]
            ),
            pltpu.make_async_copy(jac_ref.at[:, cols], held_ref.at[:, cols], jac_sem.at[step]),
        )

    for step in range(STEPS):
        for copy in copies(step):
            copy.start()

    def add(step, total):
        for copy in copies(step):
            copy.wait()
        cols = columns(step)
        return total + lax.dot_general(
            blocks_buf[:, cols].astype(jnp.bfloat16),
            held_ref[:, cols],
            (((1,), (1,)), ((), ())),
            preferred_element_type=jnp.float32,
        )

    out_ref[...] = lax.fori_loop(0, STEPS, add, jnp.zeros(out_ref.shape, jnp.float32))


def predict(me, blocks, jacobian):
    k, ncols = blocks.shape
    rows = jacobian.shape[0]
    return pl.pallas_call(
        predict_kernel,
        in_specs=[SMEM, HBM, HBM],
        out_specs=[VMEM, VMEM],
        out_shape=[
            pltpu.VMEM((k, rows), jnp.float32),
            pltpu.VMEM(jacobian.shape, jacobian.dtype),
        ],
        scratch_shapes=[
            pltpu.VMEM((k, ncols), jnp.float32),
            pltpu.SemaphoreType.DMA((STEPS,)),
            pltpu.SemaphoreType.DMA((STEPS,)),
        ],
        compiler_params=pltpu.CompilerParams(vmem_limit_bytes=48 * MIB),
        cost_estimate=pl.CostEstimate(
            flops=2 * k * ncols * rows, bytes_accessed=2 * rows * ncols, transcendentals=0
        ),
    )(me, blocks, jacobian)


def product(me, weighted, held, other_core, slots, stream, *after):
    k, rows = weighted.shape
    width = held.shape[1] // (N_CORE * SLOTS * STREAMS)

    def kernel(me_ref, weighted_ref, held_ref, *refs):
        out_ref = refs[-1]
        core = lax.rem(me_ref[0], N_CORE)
        core = 1 - core if other_core else core
        for i, slot in enumerate(slots):
            out_ref[i] = jnp.dot(
                weighted_ref[...],
                held_ref[:, slot_columns(me_ref[0], core, slot, stream, width)],
                preferred_element_type=jnp.float32,
            )

    return pl.pallas_call(
        kernel,
        in_specs=[SMEM, VMEM, VMEM] + [ANY] * len(after),
        out_specs=VMEM,
        out_shape=jax.ShapeDtypeStruct((len(slots), k, width), jnp.float32),
        compiler_params=pltpu.CompilerParams(vmem_limit_bytes=24 * MIB),
        cost_estimate=pl.CostEstimate(
            flops=2 * k * len(slots) * width * rows,
            bytes_accessed=2 * rows * len(slots) * width,
            transcendentals=0,
        ),
    )(me, weighted, held, *after)


def assemble(me, streams, ncols):
    k, width = streams[0][0].shape[-2:]
    per_stream = len(streams[0])

    def kernel(me_ref, *refs):
        out_ref = refs[-1]
        core = lax.rem(me_ref[0], N_CORE)
        for stream in range(STREAMS):
            parts = refs[stream * per_stream : (stream + 1) * per_stream]
            for owner, (low, high) in ((core, parts[:2]), (1 - core, parts[2:])):
                for slot in range(SLOTS):
                    ref = low if slot < 2 else high
                    cols = slot_columns(me_ref[0], owner, slot, stream, width)
                    out_ref[:, cols] = ref[slot % 2]

    operands = [part for parts in streams for part in parts]
    return pl.pallas_call(
        kernel,
        in_specs=[SMEM] + [VMEM] * len(operands),
        out_specs=VMEM,
        out_shape=jax.ShapeDtypeStruct((k, ncols), jnp.float32),
        compiler_params=pltpu.CompilerParams(vmem_limit_bytes=16 * MIB),
    )(me, *operands)


def local(jacobian, weights, blocks):
    p, k, ncols = blocks.shape
    me = lax.axis_index("sens").astype(jnp.int32).reshape(1)

    def swap(value, pairs):
        return lax.ppermute(value, "sens", pairs)

    predicted, held = predict(me, blocks.reshape(p * k, ncols), jacobian)
    def flip(value, bits):
        return lax.ppermute(value, "cand", [(c, c ^ bits) for c in range(N_CAND)])

    predicted = predicted + flip(predicted, 1) + (flip(predicted, 3) + flip(predicted, 2))
    predicted = predicted + flip(predicted, 4)
    weighted = weights[:, None, :] * predicted.reshape(p, k, -1)
    weighted = weighted.reshape(p * k, -1).astype(jnp.bfloat16)

    highs = []
    for stream in range(STREAMS):
        high = swap(product(me, weighted, held, True, (2, 3), stream), CORE_SWAP)
        highs.append(high + product(me, weighted, held, False, (2, 3), stream))
    streams = []
    for stream in range(STREAMS):
        first, second = (X_SWAP, NEAR) if X_FIRST[stream] else (NEAR, X_SWAP)
        high = swap(highs[stream], first)
        low = swap(product(me, weighted, held, True, (0, 1), stream, highs[-1]), CORE_SWAP)
        low = low + product(me, weighted, held, False, (0, 1), stream, highs[-1])
        total = low[0] + high[0] + swap(low[1] + high[1], second)
        for pairs in SUMS[stream]:
            total = total + swap(total, pairs)
        own = swap(total, first)
        other = swap(total, second)
        low = jnp.stack([total, other])
        high = jnp.stack([own, swap(other, first)])
        streams.append((low, high, swap(low, CORE_SWAP), swap(high, CORE_SWAP)))
    return assemble(me, streams, ncols).reshape(p, k, ncols)


def solution(mesh):
    return jax.shard_map(
        local,
        mesh=mesh,
        in_specs=(P("sens", "cand"), P(None, "sens"), P(None, None, "cand")),
        out_specs=P(None, None, "cand"),
        check_vma=False,
    )
```

```python
import jax
import jax.numpy as jnp
from jax import lax
from jax.experimental import pallas as pl
from jax.experimental.pallas import tpu as pltpu
from jax.sharding import PartitionSpec as P

N_CORE = 2
N_Z = 8
N_SENS = 32
N_CAND = 8
SLOTS = 4
STREAMS = 2
STEPS = 8
MIB = 1 << 20

STEP_OF_EVEN = (1, -1, 3)


def z_pairs(stage):
    pairs = []
    for s in range(N_SENS):
        core, z, xl = s % N_CORE, (s // N_CORE) % N_Z, s // (N_CORE * N_Z)
        sign = 1 if (z - core) % 2 == 0 else -1
        to = (z + sign * STEP_OF_EVEN[stage]) % N_Z
        pairs.append((s, (xl * N_Z + to) * N_CORE + core))
    return pairs


NEAR, NEXT, FAR = z_pairs(0), z_pairs(1), z_pairs(2)
CORE_SWAP = [(s, s ^ 1) for s in range(N_SENS)]
X_SWAP = [(s, s ^ 16) for s in range(N_SENS)]
CAND_STAGES = [[(c, c ^ flip) for c in range(N_CAND)] for flip in (1, 3, 4)]
X_FIRST = (False, False)
SUMS = ((FAR, NEXT), (NEXT, FAR))

VMEM = pl.BlockSpec(memory_space=pltpu.VMEM)
SMEM = pl.BlockSpec(memory_space=pltpu.SMEM)
HBM = pl.BlockSpec(memory_space=pltpu.HBM)
ANY = pl.BlockSpec(memory_space=pl.ANY)


def slot_columns(me, core, slot, stream, width):
    place = lax.rem(lax.div(me, N_CORE) + N_Z - core, N_Z)
    half = lax.rem(lax.div(place + 1, 2), 2)
    xl = lax.div(me, N_CORE * N_Z)
    first, second = slot // 2, slot % 2
    if X_FIRST[stream]:
        first, second = second, first
    half = 1 - half if first else half
    xl = 1 - xl if second else xl
    block = (core * STREAMS + stream) * SLOTS + 2 * half + xl
    return pl.ds(pl.multiple_of(block * width, width), width)


def predict_kernel(
    me_ref, blocks_ref, jac_ref, out_ref, held_ref, blocks_buf, blocks_sem, jac_sem
):
    width = jac_ref.shape[1] // STEPS

    def columns(step):
        return pl.ds(pl.multiple_of(step * width, width), width)

    def copies(step):
        cols = columns(step)
        return (
            pltpu.make_async_copy(
                blocks_ref.at[:, cols], blocks_buf.at[:, cols], blocks_sem.at[step]
            ),
            pltpu.make_async_copy(jac_ref.at[:, cols], held_ref.at[:, cols], jac_sem.at[step]),
        )

    for step in range(STEPS):
        for copy in copies(step):
            copy.start()

    def add(step, total):
        for copy in copies(step):
            copy.wait()
        cols = columns(step)
        return total + lax.dot_general(
            held_ref[:, cols],
            blocks_buf[:, cols].astype(jnp.bfloat16),
            (((1,), (1,)), ((), ())),
            preferred_element_type=jnp.float32,
        )

    out_ref[...] = lax.fori_loop(0, STEPS, add, jnp.zeros(out_ref.shape[::-1], jnp.float32)).T


def predict(me, blocks, jacobian):
    k, ncols = blocks.shape
    rows = jacobian.shape[0]
    return pl.pallas_call(
        predict_kernel,
        in_specs=[SMEM, HBM, HBM],
        out_specs=[VMEM, VMEM],
        out_shape=[
            pltpu.VMEM((k, rows), jnp.float32),
            pltpu.VMEM(jacobian.shape, jacobian.dtype),
        ],
        scratch_shapes=[
            pltpu.VMEM((k, ncols), jnp.float32),
            pltpu.SemaphoreType.DMA((STEPS,)),
            pltpu.SemaphoreType.DMA((STEPS,)),
        ],
        compiler_params=pltpu.CompilerParams(vmem_limit_bytes=48 * MIB),
        cost_estimate=pl.CostEstimate(
            flops=2 * k * ncols * rows, bytes_accessed=2 * rows * ncols, transcendentals=0
        ),
    )(me, blocks, jacobian)


def product(me, weighted, held, other_core, slots, stream, *after):
    k, rows = weighted.shape
    width = held.shape[1] // (N_CORE * SLOTS * STREAMS)

    def kernel(me_ref, weighted_ref, held_ref, *refs):
        out_ref = refs[-1]
        core = lax.rem(me_ref[0], N_CORE)
        core = 1 - core if other_core else core
        for i, slot in enumerate(slots):
            out_ref[i] = jnp.dot(
                weighted_ref[...],
                held_ref[:, slot_columns(me_ref[0], core, slot, stream, width)],
                preferred_element_type=jnp.float32,
            )

    return pl.pallas_call(
        kernel,
        in_specs=[SMEM, VMEM, VMEM] + [ANY] * len(after),
        out_specs=VMEM,
        out_shape=jax.ShapeDtypeStruct((len(slots), k, width), jnp.float32),
        compiler_params=pltpu.CompilerParams(vmem_limit_bytes=24 * MIB),
        cost_estimate=pl.CostEstimate(
            flops=2 * k * len(slots) * width * rows,
            bytes_accessed=2 * rows * len(slots) * width,
            transcendentals=0,
        ),
    )(me, weighted, held, *after)


def assemble(me, streams, ncols):
    k, width = streams[0][0].shape[-2:]
    per_stream = len(streams[0])

    def kernel(me_ref, *refs):
        out_ref = refs[-1]
        core = lax.rem(me_ref[0], N_CORE)
        for stream in range(STREAMS):
            parts = refs[stream * per_stream : (stream + 1) * per_stream]
            for owner, (low, high) in ((core, parts[:2]), (1 - core, parts[2:])):
                for slot in range(SLOTS):
                    ref = low if slot < 2 else high
                    cols = slot_columns(me_ref[0], owner, slot, stream, width)
                    out_ref[:, cols] = ref[slot % 2]

    operands = [part for parts in streams for part in parts]
    return pl.pallas_call(
        kernel,
        in_specs=[SMEM] + [VMEM] * len(operands),
        out_specs=VMEM,
        out_shape=jax.ShapeDtypeStruct((k, ncols), jnp.float32),
        compiler_params=pltpu.CompilerParams(vmem_limit_bytes=16 * MIB),
    )(me, *operands)


def local(jacobian, weights, blocks):
    p, k, ncols = blocks.shape
    me = lax.axis_index("sens").astype(jnp.int32).reshape(1)

    def swap(value, pairs):
        return lax.ppermute(value, "sens", pairs)

    predicted, held = predict(me, blocks.reshape(p * k, ncols), jacobian)
    def flip(value, bits):
        return lax.ppermute(value, "cand", [(c, c ^ bits) for c in range(N_CAND)])

    predicted = predicted + flip(predicted, 1) + (flip(predicted, 3) + flip(predicted, 2))
    predicted = predicted + flip(predicted, 4)
    weighted = weights[:, None, :] * predicted.reshape(p, k, -1)
    weighted = weighted.reshape(p * k, -1).astype(jnp.bfloat16)

    highs = []
    for stream in range(STREAMS):
        high = swap(product(me, weighted, held, True, (2, 3), stream), CORE_SWAP)
        highs.append(high + product(me, weighted, held, False, (2, 3), stream))
    streams = []
    for stream in range(STREAMS):
        first, second = (X_SWAP, NEAR) if X_FIRST[stream] else (NEAR, X_SWAP)
        high = swap(highs[stream], first)
        low = swap(product(me, weighted, held, True, (0, 1), stream, highs[-1]), CORE_SWAP)
        low = low + product(me, weighted, held, False, (0, 1), stream, highs[-1])
        total = low[0] + high[0] + swap(low[1] + high[1], second)
        for pairs in SUMS[stream]:
            total = total + swap(total, pairs)
        own = swap(total, first)
        other = swap(total, second)
        low = jnp.stack([total, other])
        high = jnp.stack([own, swap(other, first)])
        streams.append((low, high, swap(low, CORE_SWAP), swap(high, CORE_SWAP)))
    return assemble(me, streams, ncols).reshape(p, k, ncols)


def solution(mesh):
    return jax.shard_map(
        local,
        mesh=mesh,
        in_specs=(P("sens", "cand"), P(None, "sens"), P(None, None, "cand")),
        out_specs=P(None, None, "cand"),
        check_vma=False,
    )
```
